512 devices in a mesh: lat: 128 (over z, y, core), rad: 4 (over x).
Axes of the slice: x: 4, y: 8, z: 8, core: 2. Of those that a mesh axis runs over, the one named last changes fastest.
Arguments:
- displacement: float32 [64, 98304], P('rad', 'lat'), may hold values from -6 to 6
- surface_load: float32 [64, 98304], P('rad', 'lat'), may hold values from -6 to 6
- dens_grad: float32 [64, 98304], P('rad', 'lat'), may hold values from 0.5 to 2
- dens_ref: float32 [64], P('rad'), may hold values from 0.5 to 2
- relax_rate: float32 [64, 98304], P('rad', 'lat'), may hold values from 0.02 to 0.2
- basis: bfloat16 [2432, 98304], P(None, 'lat'), may hold values from -0.078125 to 0.078125
- neighbours: int32 [4, 98304], P(None, 'lat'), may hold values from 0 to 767
- green: float32 [49, 64, 64], replicated, may hold values from -6 to 6
Outputs:
- relaxed: float32 [64, 98304], P('rad', 'lat')
- step_sizes: float32 [3], replicated
The draws below stay inside these ranges and needn't reach their ends.
Inputs may be any that keep to these rules, and one draw needn't show every extreme that they name: `neighbours`: indices of columns inside the same tile of 768 columns.
All inputs are finite; a program needn't handle non-finite values.
Results may differ from the reference program's by a relative error of at most 0.0045.
Values may be sent and summed in bfloat16 or wider, within the bound.
A program may use at most 64 MiB of HBM per device.

```python
import math
import jax
import jax.numpy as jnp
from jax import lax

DEG = 48
L = 64
C_DEV = 768
ITERS = 3
KH = 2401
KP = 2432
C_TOTAL = 98304


def plant(result, stream_key, low, largest):
    extent = result.shape
    place = [jax.random.randint(jax.random.fold_in(stream_key, axis), (), 0, extent[axis]) for axis in range(len(extent))]
    result = result.at[tuple(place)].set(low)
    longest = extent.index(max(extent))
    place[longest] = (place[longest] + 1) % extent[longest]
    return result.at[tuple(place)].set(largest)


def raised(result, rng, source, target, shards_of, factor):
    def block_of(position):
        return (jnp.arange(result.shape[position]) // (result.shape[position] // shards_of)).reshape((-1,) + (1,) * (result.ndim - 1 - position))

    one_side = jax.random.permutation(rng, shards_of)[block_of(target)]
    second = (block_of(target) + shards_of // 2) % shards_of
    return jnp.where((block_of(source) == one_side) | (block_of(source) == second), factor * result, result)


def shard_levels(rng, dims, shards, smallest, largest):
    loudness, own = 1.0, jax.random.fold_in(rng, 6)
    for position, shards_of in shards:
        heights = jnp.exp(jax.random.uniform(jax.random.fold_in(own, position), (shards_of,), jnp.float32, smallest / len(shards), largest / len(shards)))
        loudness = loudness * jnp.repeat(heights, dims[position] // shards_of).reshape([-1 if axis == position else 1 for axis in range(len(dims))])
    return loudness


def noise(own_key, dims, deviation, reach, shards=(), kind=jnp.bfloat16):
    array = deviation * jax.random.normal(own_key, dims, jnp.float32)
    if shards:
        array = array * shard_levels(own_key, dims, shards, -0.22, 0.18)
    return jnp.clip(array, -reach, reach).astype(kind)


def bell_draw_with(own_key, extent, width, most, cuts, heavy, held_as=jnp.bfloat16):
    values = width * jax.random.normal(own_key, extent, jnp.float32)
    if cuts:
        values = values * shard_levels(own_key, extent, cuts, -0.22, 0.18)
    return jnp.clip(raised(values, jax.random.fold_in(own_key, 3), *heavy), -most, most).astype(held_as)


def setup_inputs(seed: int = 0) -> dict:
    key_of = jax.random.split(jax.random.key(seed), 9)
    return {
        "displacement": noise(key_of[0], (L, C_TOTAL), 1.0, 6.0, ((0, 4), (1, 128)), jnp.float32),
        "surface_load": noise(key_of[1], (L, C_TOTAL), 1.0, 6.0, ((0, 4), (1, 128)), jnp.float32),
        "dens_grad": jnp.clip(jnp.exp(math.log(2.0) - 1.3862944 * jax.random.uniform(key_of[2], (L, C_TOTAL), jnp.float32) ** shard_levels(key_of[2], (L, C_TOTAL), ((0, 4), (1, 128)), -0.2, 0.2)), 0.5, 2.0),
        "dens_ref": jnp.clip(0.5 + 1.5 * jax.random.uniform(key_of[3], (L,), jnp.float32) ** shard_levels(key_of[3], (L,), ((0, 4),), -0.2, 0.2), 0.5, 2.0),
        "relax_rate": jnp.clip(jnp.exp(math.log(0.2) - 2.3025851 * jax.random.uniform(key_of[4], (L, C_TOTAL), jnp.float32) ** shard_levels(key_of[4], (L, C_TOTAL), ((0, 4), (1, 128)), -0.2, 0.2)), 0.02, 0.2),
        "basis": bell_draw_with(key_of[5], (KP, C_TOTAL), C_TOTAL ** -0.5, 0.078125, ((1, 128),), (1, 0, 128, 5.5)),
        "neighbours": plant(jax.random.randint(key_of[6], (4, C_TOTAL), 0, C_DEV), jax.random.fold_in(key_of[6], 1), 0, C_DEV - 1).astype(jnp.int32),
        "green": noise(key_of[7], (DEG + 1, L, L), (max(1, L * KP // (4 * C_TOTAL))) ** -0.5, 6.0, (), jnp.float32),
    }


def radial_step(field):
    padded = jnp.pad(field, ((1, 1), (0, 0)))
    return (padded[2:] - padded[:-2]) * 0.5

def apply_degrees(coefs, green):
    blocks = []
    for degree in range(DEG + 1):
        rows = coefs[degree * degree:(degree + 1) * (degree + 1)]
        blocks.append(lax.dot_general(rows, green[degree], (((1,), (1,)), ((), ())), precision=lax.Precision.HIGHEST, preferred_element_type=jnp.float32))
    blocks.append(jnp.zeros((KP - KH, green.shape[1]), jnp.float32))
    return jnp.concatenate(blocks, axis=0)

def reference(displacement, surface_load, dens_grad, dens_ref, relax_rate, basis, neighbours, green):
    u = displacement
    tile_start = jnp.arange(C_TOTAL, dtype=jnp.int32) // C_DEV * C_DEV
    global_idx = tile_start[None, :] + neighbours
    sizes = []
    for it in range(ITERS):
        rho = (dens_grad * u + dens_ref[:, None] * radial_step(u)).astype(jnp.bfloat16)
        coefs = lax.dot_general(basis, rho, (((1,), (1,)), ((), ())), preferred_element_type=jnp.float32)
        phi = apply_degrees(coefs, green).astype(jnp.bfloat16)
        potential = lax.dot_general(phi, basis, (((0,), (0,)), ((), ())), preferred_element_type=jnp.float32)
        force = radial_step(potential)
        lap = lax.optimization_barrier(jnp.sum(u[:, global_idx], axis=1)) - 4.0 * u
        new = u + relax_rate * (surface_load + force + lap - u)
        sizes.append(jnp.sqrt(jnp.sum((new - u) ** 2) / (L * C_TOTAL)))
        u = new
    return (u, jnp.stack(sizes))
```

```python
import functools

import jax
import jax.numpy as jnp
from jax import lax
from jax.experimental import pallas as pl
from jax.experimental.pallas import tpu as pltpu
from jax.sharding import Mesh
from jax.sharding import PartitionSpec as P

DEG = 48
L = 64
ITERS = 3
KH = 2401
NZ, NY, NC, NX = 8, 8, 2, 4
GROUPS = 19
LANES = 128
AXES = ("lz", "ly", "lc", "rad")
LAT = AXES[:3]
MESH = pl.DeviceIdType.MESH
NT = (((1,), (1,)), ((), ()))
NN = (((1,), (0,)), ((), ()))
F32 = jnp.float32
BF16 = jnp.bfloat16

PLANE = sorted(
    [(dz, dy) for dz in range(NZ) for dy in range(NY) if dz or dy],
    key=lambda o: -(min(o[0], NZ - o[0]) + min(o[1], NY - o[1])),
)


def group_chip(g):
    if g < 8:
        return g, g % 4
    if g < 16:
        return g - 8, (g - 8 + 2) % 4
    return (g - 16) * 3, ((g - 16) * 3 + 1) % 4


def owned_group(z, y, core):
    b = y // 2
    g = jnp.where(b == z % 4, z, -1)
    g = jnp.where(b == (z + 2) % 4, z + 8, g)
    extra = (b == (z + 1) % 4) & (z % 3 == 0)
    g = jnp.where(extra, z // 3 + 16, g)
    return jnp.where(y % 2 == core, g, -1)


def kernel(
    disp, load, grad, dref, rate, basis_hbm, nbr, green_hbm,
    out, sizes,
    basis, green, u_s, ld_s, rt_s, gr_s, nbr_s, dref_s, hsend, hrecv, count, gexp, onehot,
    base, part, rsbuf, xsend, xbuf, lsend, lbuf, fsend, fplane, fsend2, fx, sq_s,
    in_sem, hs_sem, hr_sem, rs_ssem, rs_rsem, x_ssem, x_rsem, ag_ssem, ag_rsem,
    f_ssem, f_rsem, f2_ssem, f2_rsem,
):
    z, y, c, x = (lax.axis_index(a) for a in AXES)
    chip = z * NY + y
    g_own = owned_group(z, y, c)
    owner = g_own >= 0
    other_y = 2 * (y // 2) + (1 - y % 2)

    plane_ids = [((z + dz) % NZ, (y + dy) % NY, c, x) for dz, dy in PLANE]
    same = [(z, y, c, (x + d) % NX) for d in (2, 1, 3)]
    cross = [(z, other_y, 1 - c, (x + d) % NX) for d in (2, 1, 3, 0)]
    near_ids = same + cross

    barrier = pltpu.get_barrier_semaphore()
    for dev in plane_ids + near_ids:
        pl.semaphore_signal(barrier, inc=1, device_id=dev, device_id_type=MESH)

    loads = [
        pltpu.make_async_copy(nbr, nbr_s, in_sem.at[0]),
        pltpu.make_async_copy(disp, u_s.at[pl.ds(0, 16)], in_sem.at[1]),
        pltpu.make_async_copy(load, ld_s.at[pl.ds(0, 16)], in_sem.at[2]),
        pltpu.make_async_copy(rate, rt_s.at[pl.ds(0, 16)], in_sem.at[3]),
        pltpu.make_async_copy(grad, gr_s, in_sem.at[4]),
        pltpu.make_async_copy(dref, dref_s, in_sem.at[5]),
        pltpu.make_async_copy(green_hbm, green, in_sem.at[6]),
        pltpu.make_async_copy(basis_hbm, basis, in_sem.at[7]),
    ]
    for copy in loads:
        copy.start()

    loads[0].wait()

    def count_rows(block, carry):
        start = pl.multiple_of(block * 64, 64)
        rows = lax.broadcasted_iota(jnp.int32, (64, 768), 0) + start
        total = jnp.zeros((64, 768), F32)
        for j in range(4):
            total = total + jnp.where(nbr_s[j : j + 1, :] == rows, 1.0, 0.0)
        count[pl.ds(start, 64), :] = total.astype(BF16)
        return carry

    lax.fori_loop(0, 12, count_rows, 0)

    for copy in loads[1:7]:
        copy.wait()

    @pl.when(owner)
    def _():
        k = g_own * LANES + lax.broadcasted_iota(jnp.int32, (LANES, LANES), 1)
        d = lax.broadcasted_iota(jnp.int32, (LANES, LANES), 0) % 64
        hit = (k >= d * d) & (k < (d + 1) * (d + 1)) & (k < KH)
        onehot[...] = jnp.where(hit, 1.0, 0.0).astype(BF16)

        def green_row(i):
            layer = x * 16 + i
            inside = (layer >= 0) & (layer < L)
            at = jnp.where(inside, layer, 0)
            rows = green[pl.ds(at, DEG + 1, stride=L), :]
            rows = jnp.where(inside, rows, 0.0)
            return jnp.concatenate([rows, jnp.zeros((64 - DEG - 1, L), F32)], axis=0)

        def expand(slot, i):
            layer = x * 16 + i
            inside = (layer >= 0) & (layer < L)
            diff = (green_row(i + 1) - green_row(i - 1)) * 0.5
            diff = jnp.where(inside, diff, 0.0).T
            high = diff.astype(BF16).astype(F32)
            both = jnp.concatenate([high, diff - high], axis=1).astype(BF16)
            gexp[slot] = lax.dot_general(both, onehot[...], NN, preferred_element_type=F32)

        def expand_main(i, carry):
            expand(i, i)
            return carry

        lax.fori_loop(0, 16, expand_main, 0)
        expand(16, -1)
        expand(17, 16)

    zeros5 = jnp.zeros((5, 768), F32)
    hsend[0] = jnp.concatenate([u_s[15:16], ld_s[15:16], rt_s[15:16], zeros5], axis=0)
    hsend[1] = jnp.concatenate([u_s[0:1], ld_s[0:1], rt_s[0:1], zeros5], axis=0)

    pl.semaphore_wait(barrier, len(plane_ids) + len(near_ids))

    halos = []
    for side, step in ((0, 1), (1, NX - 1)):
        halos.append(
            pltpu.make_async_remote_copy(
                src_ref=hsend.at[side], dst_ref=hrecv.at[side],
                send_sem=hs_sem.at[side], recv_sem=hr_sem.at[side],
                device_id=(z, y, c, (x + step) % NX), device_id_type=MESH,
            )
        )
    for copy in halos:
        copy.start()
    loads[7].wait()
    eye = lax.broadcasted_iota(jnp.int32, (16, 16), 0) == lax.broadcasted_iota(jnp.int32, (16, 16), 1)
    half_ref = 0.5 * jnp.sum(jnp.where(eye, dref_s[...], 0.0), axis=1, keepdims=True)
    for copy in halos:
        copy.wait()
    before = jnp.where(x > 0, hrecv[0], 0.0)
    after = jnp.where(x < NX - 1, hrecv[1], 0.0)
    zeros6 = jnp.zeros((6, 768), F32)
    for row, ref in enumerate((u_s, ld_s, rt_s)):
        ref[16:24] = jnp.concatenate([before[row : row + 1], after[row : row + 1], zeros6], axis=0)

    def step(it, carry):
        u = u_s[...]
        inner = u[0:16]
        upper = jnp.concatenate([u[1:16], u[17:18]], axis=0)
        lower = jnp.concatenate([u[16:17], u[0:15]], axis=0)
        rho = (gr_s[...] * inner + half_ref * (upper - lower)).astype(BF16)

        for g in range(GROUPS):
            tile = lax.dot_general(
                rho, basis[g * LANES : (g + 1) * LANES, :], NT, preferred_element_type=F32
            )
            part[it, g] = tile.astype(BF16)
            gz, gb = group_chip(g)
            gy = gb * 2 + c

            @pl.when(g_own != g)
            def _():
                pltpu.make_async_remote_copy(
                    src_ref=part.at[it, g], dst_ref=rsbuf.at[it, chip],
                    send_sem=rs_ssem.at[it], recv_sem=rs_rsem.at[it],
                    device_id=(gz, gy, c, x), device_id_type=MESH,
                ).start()

            @pl.when(g_own == g)
            def _():
                rsbuf[it, chip] = tile.astype(BF16)

        high = u.astype(BF16).astype(F32)
        halves = jnp.concatenate([high, u - high], axis=0).astype(BF16)
        gathered = lax.dot_general(halves, count[...], NN, preferred_element_type=F32)
        lap = gathered[0:24] + gathered[24:48] - 4.0 * u
        base[...] = ld_s[...] + lap - u

        @pl.when(owner)
        def _():
            incoming = rsbuf.at[it, pl.ds(0, NZ * NY - 1)]
            pltpu.make_async_copy(incoming, incoming, rs_rsem.at[it]).wait()
            sums = [jnp.zeros((16, LANES), F32) for _ in range(4)]
            for s in range(NZ * NY):
                sums[s % 4] = sums[s % 4] + rsbuf[it, s].astype(F32)
            total = (sums[0] + sums[1]) + (sums[2] + sums[3])
            xsend[it] = total
            me = x * NC + c
            for dev in near_ids:
                pltpu.make_async_remote_copy(
                    src_ref=xsend.at[it], dst_ref=xbuf.at[it, me],
                    send_sem=x_ssem.at[it], recv_sem=x_rsem.at[it],
                    device_id=dev, device_id_type=MESH,
                ).start()
            xbuf[it, me] = total
            others = xbuf.at[it, pl.ds(0, NX * NC - 1)]
            pltpu.make_async_copy(others, others, x_rsem.at[it]).wait()
            coefs = jnp.concatenate(
                [xbuf[it, 2 * b] + xbuf[it, 2 * b + 1] for b in range(NX)], axis=0
            )
            rows = [jnp.sum(gexp[i] * coefs, axis=0, keepdims=True) for i in range(18)]
            rows.append(jnp.zeros((14, LANES), F32))
            phi = jnp.concatenate(rows, axis=0).astype(BF16)
            lsend[it] = phi
            for dev in plane_ids:
                pltpu.make_async_remote_copy(
                    src_ref=lsend.at[it], dst_ref=lbuf.at[it, g_own],
                    send_sem=ag_ssem.at[it], recv_sem=ag_rsem.at[it, g_own],
                    device_id=dev, device_id_type=MESH,
                ).start()
            lbuf[it, g_own] = phi

        force = jnp.zeros((32, 768), F32)
        for g in range(GROUPS):
            @pl.when(g_own != g)
            def _():
                pltpu.make_async_copy(lbuf.at[it, g], lbuf.at[it, g], ag_rsem.at[it, g]).wait()

            force = force + lax.dot_general(
                lbuf[it, g], basis[g * LANES : (g + 1) * LANES, :], NN, preferred_element_type=F32
            )
        delta = rt_s[...] * (base[...] + force[0:24])
        u_s[...] = u_s[...] + delta
        square = delta[0:16] * delta[0:16]
        square = jnp.sum(jnp.sum(square, axis=0, keepdims=True), axis=1, keepdims=True)
        lane = lax.broadcasted_iota(jnp.int32, (1, LANES), 1)
        sq_s[...] = jnp.where(lane == it, square, sq_s[...])
        return carry

    sq_s[...] = jnp.zeros((1, LANES), F32)
    lax.fori_loop(0, ITERS, step, 0)

    fsend[0] = sq_s[...]
    for dev in plane_ids:
        pltpu.make_async_remote_copy(
            src_ref=fsend.at[0], dst_ref=fplane.at[chip], send_sem=f_ssem, recv_sem=f_rsem,
            device_id=dev, device_id_type=MESH,
        ).start()
    fplane[chip] = sq_s[...]
    out[...] = u_s[0:16]
    others = fplane.at[pl.ds(0, NZ * NY - 1)]
    pltpu.make_async_copy(others, others, f_rsem).wait()
    total = jnp.zeros((1, LANES), F32)
    for s in range(NZ * NY):
        total = total + fplane[s]
    fsend2[0] = total
    me = x * NC + c
    for dev in near_ids:
        pltpu.make_async_remote_copy(
            src_ref=fsend2.at[0], dst_ref=fx.at[me], send_sem=f2_ssem, recv_sem=f2_rsem,
            device_id=dev, device_id_type=MESH,
        ).start()
    fx[me] = total
    others2 = fx.at[pl.ds(0, NX * NC - 1)]
    pltpu.make_async_copy(others2, others2, f2_rsem).wait()
    total = jnp.zeros((1, LANES), F32)
    for s in range(NX * NC):
        total = total + fx[s]
    sizes[...] = jnp.sqrt(total * (1.0 / (L * 768 * NZ * NY * NC)))

    pltpu.make_async_copy(others, others, f_ssem).wait()
    pltpu.make_async_copy(others2, others2, f2_ssem).wait()
    for it in range(ITERS):
        @pl.when(owner)
        def _():
            sent = part.at[it, pl.ds(0, GROUPS - 1)]
            pltpu.make_async_copy(sent, sent, rs_ssem.at[it]).wait()
            sent = xbuf.at[it, pl.ds(0, NX * NC - 1)]
            pltpu.make_async_copy(sent, sent, x_ssem.at[it]).wait()
            sent = rsbuf.at[pl.ds(0, 2), pl.ds(0, NZ * NY - 1)]
            pltpu.make_async_copy(sent, sent, ag_ssem.at[it]).wait()

        @pl.when(jnp.logical_not(owner))
        def _():
            sent = part.at[it]
            pltpu.make_async_copy(sent, sent, rs_ssem.at[it]).wait()


def local(displacement, surface_load, dens_grad, dens_ref, relax_rate, basis, neighbours, green):
    vmem = pltpu.VMEM
    dma = pltpu.SemaphoreType.DMA
    scratch = [
        vmem((2432, 768), BF16),
        vmem(((DEG + 1) * L, L), F32),
        vmem((24, 768), F32),
        vmem((24, 768), F32),
        vmem((24, 768), F32),
        vmem((16, 768), F32),
        vmem((4, 768), jnp.int32),
        vmem((1, 16), F32),
        vmem((2, 8, 768), F32),
        vmem((2, 8, 768), F32),
        vmem((768, 768), BF16),
        vmem((18, 64, LANES), F32),
        vmem((LANES, LANES), BF16),
        vmem((24, 768), F32),
        vmem((ITERS, GROUPS, 16, LANES), BF16),
        vmem((ITERS, NZ * NY, 16, LANES), BF16),
        vmem((ITERS, 16, LANES), F32),
        vmem((ITERS, NX * NC, 16, LANES), F32),
        vmem((ITERS, 32, LANES), BF16),
        vmem((ITERS, GROUPS, 32, LANES), BF16),
        vmem((1, 1, LANES), F32),
        vmem((NZ * NY, 1, LANES), F32),
        vmem((1, 1, LANES), F32),
        vmem((NX * NC, 1, LANES), F32),
        vmem((1, LANES), F32),
        dma((8,)), dma((2,)), dma((2,)),
        dma((ITERS,)), dma((ITERS,)), dma((ITERS,)), dma((ITERS,)), dma((ITERS,)),
        dma((ITERS, GROUPS)),
        dma, dma, dma, dma,
    ]
    relaxed, sizes = pl.pallas_call(
        kernel,
        out_shape=(
            jax.ShapeDtypeStruct((16, 768), F32),
            jax.ShapeDtypeStruct((1, LANES), F32),
        ),
        in_specs=[pl.BlockSpec(memory_space=pl.ANY)] * 8,
        out_specs=(
            pl.BlockSpec(memory_space=pltpu.VMEM),
            pl.BlockSpec(memory_space=pltpu.VMEM),
        ),
        scratch_shapes=scratch,
        compiler_params=pltpu.CompilerParams(
            collective_id=0, has_side_effects=True, vmem_limit_bytes=56 << 20
        ),
        name="relaxation",
    )(
        displacement,
        surface_load,
        dens_grad,
        dens_ref.reshape(1, 16),
        relax_rate,
        basis,
        neighbours,
        green.reshape((DEG + 1) * L, L),
    )
    return relaxed, sizes[0, :ITERS]


def solution(mesh):
    torus = Mesh(mesh.devices.reshape(NZ, NY, NC, NX), AXES)
    return jax.shard_map(
        local,
        mesh=torus,
        in_specs=(
            P("rad", LAT),
            P("rad", LAT),
            P("rad", LAT),
            P("rad"),
            P("rad", LAT),
            P(None, LAT),
            P(None, LAT),
            P(),
        ),
        out_specs=(P("rad", LAT), P()),
        check_vma=False,
    )
```

```python
import jax
import jax.numpy as jnp
from jax import lax
from jax.experimental import pallas as pl
from jax.experimental.pallas import tpu as pltpu
from jax.sharding import Mesh
from jax.sharding import PartitionSpec as P

DEG = 48
L = 64
ITERS = 3
KH = 2401
NZ, NY, NC, NX = 8, 8, 2, 4
GROUPS = 19
LANES = 128
AXES = ("lz", "ly", "lc", "rad")
LAT = AXES[:3]
MESH = pl.DeviceIdType.MESH
NT = (((1,), (1,)), ((), ()))
NN = (((1,), (0,)), ((), ()))
F32 = jnp.float32
BF16 = jnp.bfloat16

PLANE = sorted(
    [(dz, dy) for dz in range(NZ) for dy in range(NY) if dz or dy],
    key=lambda o: -(min(o[0], NZ - o[0]) + min(o[1], NY - o[1])),
)


def group_chip(g):
    if g < 8:
        return g, g % 4
    if g < 16:
        return g - 8, (g - 8 + 2) % 4
    return (g - 16) * 3, ((g - 16) * 3 + 1) % 4


def owned_group(z, y, core):
    b = y // 2
    g = jnp.where(b == z % 4, z, -1)
    g = jnp.where(b == (z + 2) % 4, z + 8, g)
    extra = (b == (z + 1) % 4) & (z % 3 == 0)
    g = jnp.where(extra, z // 3 + 16, g)
    return jnp.where(y % 2 == core, g, -1)


def kernel(
    disp, load, grad, dref, rate, basis_hbm, nbr, green_hbm,
    out, sizes,
    basis, green, u_s, ld_s, rt_s, gr_s, nbr_s, dref_s, count, gexp, onehot,
    base, part, edge, rsbuf, edgebuf, xsend, xbuf, lsend, lbuf, fsend, fplane, fsend2, fx, sq_s,
    in_sem, out_sem, rs_ssem, rs_rsem, e_ssem, e_rsem, x_ssem, x_rsem, ag_ssem, ag_rsem,
    f_ssem, f_rsem, f2_ssem, f2_rsem,
):
    z, y, c, x = (lax.axis_index(a) for a in AXES)
    chip = z * NY + y
    g_own = owned_group(z, y, c)
    owner = g_own >= 0
    other_y = 2 * (y // 2) + (1 - y % 2)

    plane_ids = [((z + dz) % NZ, (y + dy) % NY, c, x) for dz, dy in PLANE]
    same = [(z, y, c, (x + d) % NX) for d in (2, 1, 3)]
    cross = [(z, other_y, 1 - c, (x + d) % NX) for d in (2, 1, 3, 0)]
    near_ids = same + cross

    barrier = pltpu.get_barrier_semaphore()
    for dev in plane_ids + near_ids:
        pl.semaphore_signal(barrier, inc=1, device_id=dev, device_id_type=MESH)

    loads = [
        pltpu.make_async_copy(disp, u_s, in_sem.at[0]),
        pltpu.make_async_copy(grad, gr_s, in_sem.at[1]),
        pltpu.make_async_copy(dref, dref_s, in_sem.at[2]),
        pltpu.make_async_copy(basis_hbm, basis, in_sem.at[3]),
        pltpu.make_async_copy(nbr, nbr_s, in_sem.at[4]),
        pltpu.make_async_copy(green_hbm, green, in_sem.at[5]),
        pltpu.make_async_copy(load, ld_s, in_sem.at[6]),
        pltpu.make_async_copy(rate, rt_s, in_sem.at[7]),
    ]
    for copy in loads:
        copy.start()

    def count_rows(block, carry):
        start = pl.multiple_of(block * 64, 64)
        rows = lax.broadcasted_iota(jnp.int32, (64, 768), 0) + start
        total = jnp.zeros((64, 768), F32)
        for j in range(4):
            total = total + jnp.where(nbr_s[j : j + 1, :] == rows, 1.0, 0.0)
        count[pl.ds(start, 64), :] = total.astype(BF16)
        return carry

    def green_row(i):
        layer = x * 16 + i
        inside = (layer >= 0) & (layer < L)
        at = jnp.where(inside, layer, 0)
        rows = green[pl.ds(at, DEG + 1, stride=L), :]
        rows = jnp.where(inside, rows, 0.0)
        return jnp.concatenate([rows, jnp.zeros((64 - DEG - 1, L), F32)], axis=0)

    def expand(i, carry):
        diff = ((green_row(i + 1) - green_row(i - 1)) * 0.5).T
        high = diff.astype(BF16).astype(F32)
        both = jnp.concatenate([high, diff - high], axis=1).astype(BF16)
        gexp[i] = lax.dot_general(both, onehot[...], NN, preferred_element_type=F32)
        return carry

    for copy in loads[:4]:
        copy.wait()
    eye = lax.broadcasted_iota(jnp.int32, (16, 16), 0) == lax.broadcasted_iota(jnp.int32, (16, 16), 1)
    half_ref = 0.5 * jnp.sum(jnp.where(eye, dref_s[...], 0.0), axis=1, keepdims=True)
    ends = jnp.concatenate(
        [
            jnp.broadcast_to(half_ref[0:1], (1, LANES)),
            jnp.broadcast_to(half_ref[15:16], (1, LANES)),
            jnp.zeros((4, LANES), F32),
        ],
        axis=0,
    )
    sq_s[...] = jnp.zeros((1, LANES), F32)

    pl.semaphore_wait(barrier, len(plane_ids) + len(near_ids))

    def step(it, carry):
        u = u_s[...]
        line = jnp.zeros((1, 768), F32)
        upper = jnp.concatenate([u[1:16], line], axis=0)
        lower = jnp.concatenate([line, u[0:15]], axis=0)
        rho = gr_s[...] * u + half_ref * (upper - lower)
        lines = jnp.concatenate([rho, u[0:1], u[15:16], jnp.zeros((14, 768), F32)], axis=0)
        lines = lines.astype(BF16)

        for g in range(GROUPS):
            tile = lax.dot_general(
                lines, basis[g * LANES : (g + 1) * LANES, :], NT, preferred_element_type=F32
            )
            part[it, g] = tile[0:16].astype(BF16)
            edge[it, g] = tile[16:18]
            gz, gb = group_chip(g)
            dev = (gz, gb * 2 + c, c, x)

            @pl.when(g_own != g)
            def _():
                pltpu.make_async_remote_copy(
                    src_ref=part.at[it, g], dst_ref=rsbuf.at[it, chip],
                    send_sem=rs_ssem.at[it], recv_sem=rs_rsem.at[it],
                    device_id=dev, device_id_type=MESH,
                ).start()
                pltpu.make_async_remote_copy(
                    src_ref=edge.at[it, g], dst_ref=edgebuf.at[it, chip],
                    send_sem=e_ssem.at[it], recv_sem=e_rsem.at[it],
                    device_id=dev, device_id_type=MESH,
                ).start()

            @pl.when(g_own == g)
            def _():
                rsbuf[it, chip] = tile[0:16].astype(BF16)
                edgebuf[it, chip] = tile[16:18]

        @pl.when(it == 0)
        def _():
            for copy in loads[4:]:
                copy.wait()
            lax.fori_loop(0, 12, count_rows, 0)

            @pl.when(owner)
            def _():
                k = g_own * LANES + lax.broadcasted_iota(jnp.int32, (LANES, LANES), 1)
                d = lax.broadcasted_iota(jnp.int32, (LANES, LANES), 0) % 64
                hit = (k >= d * d) & (k < (d + 1) * (d + 1)) & (k < KH)
                onehot[...] = jnp.where(hit, 1.0, 0.0).astype(BF16)
                lax.fori_loop(0, 16, expand, 0)

        high = u.astype(BF16).astype(F32)
        halves = jnp.concatenate([high, u - high], axis=0).astype(BF16)
        gathered = lax.dot_general(halves, count[...], NN, preferred_element_type=F32)
        lap = gathered[0:16] + gathered[16:32] - 4.0 * u
        base[...] = ld_s[...] + lap - u

        @pl.when(owner)
        def _():
            incoming = rsbuf.at[it, pl.ds(0, NZ * NY - 1)]
            pltpu.make_async_copy(incoming, incoming, rs_rsem.at[it]).wait()
            sums = [jnp.zeros((16, LANES), F32) for _ in range(4)]
            for s in range(NZ * NY):
                sums[s % 4] = sums[s % 4] + rsbuf[it, s].astype(F32)
            total = (sums[0] + sums[1]) + (sums[2] + sums[3])
            edges = edgebuf.at[it, pl.ds(0, NZ * NY - 1)]
            pltpu.make_async_copy(edges, edges, e_rsem.at[it]).wait()
            sums = [jnp.zeros((2, LANES), F32) for _ in range(4)]
            for s in range(NZ * NY):
                sums[s % 4] = sums[s % 4] + edgebuf[it, s]
            edge_total = (sums[0] + sums[1]) + (sums[2] + sums[3])
            total = jnp.concatenate([total, edge_total, ends], axis=0)
            xsend[it] = total
            me = x * NC + c
            for dev in near_ids:
                pltpu.make_async_remote_copy(
                    src_ref=xsend.at[it], dst_ref=xbuf.at[it, me],
                    send_sem=x_ssem.at[it], recv_sem=x_rsem.at[it],
                    device_id=dev, device_id_type=MESH,
                ).start()
            xbuf[it, me] = total
            others = xbuf.at[it, pl.ds(0, NX * NC - 1)]
            pltpu.make_async_copy(others, others, x_rsem.at[it]).wait()
            blocks = [xbuf[it, 2 * b] + xbuf[it, 2 * b + 1] for b in range(NX)]
            rows = []
            for b in range(NX):
                first, last = jnp.zeros((1, LANES), F32), jnp.zeros((1, LANES), F32)
                if b > 0:
                    first = -0.5 * blocks[b][18:19] * blocks[b - 1][17:18]
                if b < NX - 1:
                    last = 0.5 * blocks[b][19:20] * blocks[b + 1][16:17]
                mid = jnp.zeros((14, LANES), F32)
                rows.append(blocks[b][0:16] + jnp.concatenate([first, mid, last], axis=0))
            coefs = jnp.concatenate(rows, axis=0)
            rows = [jnp.sum(gexp[i] * coefs, axis=0, keepdims=True) for i in range(16)]
            phi = jnp.concatenate(rows, axis=0).astype(BF16)
            lsend[it] = phi
            for dev in plane_ids:
                pltpu.make_async_remote_copy(
                    src_ref=lsend.at[it], dst_ref=lbuf.at[it, g_own],
                    send_sem=ag_ssem.at[it], recv_sem=ag_rsem.at[it, g_own],
                    device_id=dev, device_id_type=MESH,
                ).start()
            lbuf[it, g_own] = phi

        force = jnp.zeros((16, 768), F32)
        for g in range(GROUPS):
            @pl.when(g_own != g)
            def _():
                pltpu.make_async_copy(lbuf.at[it, g], lbuf.at[it, g], ag_rsem.at[it, g]).wait()

            force = force + lax.dot_general(
                lbuf[it, g], basis[g * LANES : (g + 1) * LANES, :], NN, preferred_element_type=F32
            )
        delta = rt_s[...] * (base[...] + force)
        u_s[...] = u_s[...] + delta
        square = delta * delta
        square = jnp.sum(jnp.sum(square, axis=0, keepdims=True), axis=1, keepdims=True)
        lane = lax.broadcasted_iota(jnp.int32, (1, LANES), 1)
        sq_s[...] = jnp.where(lane == it, square, sq_s[...])
        return carry

    lax.fori_loop(0, ITERS, step, 0)
    result = pltpu.make_async_copy(u_s, out, out_sem)
    result.start()

    fsend[0] = sq_s[...]
    for dev in plane_ids:
        pltpu.make_async_remote_copy(
            src_ref=fsend.at[0], dst_ref=fplane.at[chip], send_sem=f_ssem, recv_sem=f_rsem,
            device_id=dev, device_id_type=MESH,
        ).start()
    fplane[chip] = sq_s[...]
    others = fplane.at[pl.ds(0, NZ * NY - 1)]
    pltpu.make_async_copy(others, others, f_rsem).wait()
    total = jnp.zeros((1, LANES), F32)
    for s in range(NZ * NY):
        total = total + fplane[s]
    fsend2[0] = total
    me = x * NC + c
    for dev in near_ids:
        pltpu.make_async_remote_copy(
            src_ref=fsend2.at[0], dst_ref=fx.at[me], send_sem=f2_ssem, recv_sem=f2_rsem,
            device_id=dev, device_id_type=MESH,
        ).start()
    fx[me] = total
    others2 = fx.at[pl.ds(0, NX * NC - 1)]
    pltpu.make_async_copy(others2, others2, f2_rsem).wait()
    total = jnp.zeros((1, LANES), F32)
    for s in range(NX * NC):
        total = total + fx[s]
    sizes[...] = jnp.sqrt(total * (1.0 / (L * 768 * NZ * NY * NC)))

    result.wait()
    pltpu.make_async_copy(others, others, f_ssem).wait()
    pltpu.make_async_copy(others2, others2, f2_ssem).wait()
    for it in range(ITERS):
        @pl.when(owner)
        def _():
            sent = part.at[it, pl.ds(0, GROUPS - 1)]
            pltpu.make_async_copy(sent, sent, rs_ssem.at[it]).wait()
            sent = xbuf.at[it, pl.ds(0, NX * NC - 1)]
            pltpu.make_async_copy(sent, sent, x_ssem.at[it]).wait()
            sent = edge.at[it, pl.ds(0, GROUPS - 1)]
            pltpu.make_async_copy(sent, sent, e_ssem.at[it]).wait()
            sent = rsbuf.at[0, pl.ds(0, NZ * NY - 1)]
            pltpu.make_async_copy(sent, sent, ag_ssem.at[it]).wait()

        @pl.when(jnp.logical_not(owner))
        def _():
            sent = part.at[it]
            pltpu.make_async_copy(sent, sent, rs_ssem.at[it]).wait()
            sent = edge.at[it]
            pltpu.make_async_copy(sent, sent, e_ssem.at[it]).wait()


def finish(u, row, relaxed, sizes, sem):
    copy = pltpu.make_async_copy(u, relaxed, sem)
    copy.start()
    sizes[...] = row[:, 0:ITERS]
    copy.wait()


def local(displacement, surface_load, dens_grad, dens_ref, relax_rate, basis, neighbours, green):
    vmem = pltpu.VMEM
    dma = pltpu.SemaphoreType.DMA
    scratch = [
        vmem((2432, 768), BF16),
        vmem(((DEG + 1) * L, L), F32),
        vmem((16, 768), F32),
        vmem((16, 768), F32),
        vmem((16, 768), F32),
        vmem((16, 768), F32),
        vmem((4, 768), jnp.int32),
        vmem((1, 16), F32),
        vmem((768, 768), BF16),
        vmem((16, 64, LANES), F32),
        vmem((LANES, LANES), BF16),
        vmem((16, 768), F32),
        vmem((ITERS, GROUPS, 16, LANES), BF16),
        vmem((ITERS, GROUPS, 2, LANES), F32),
        vmem((ITERS, NZ * NY, 16, LANES), BF16),
        vmem((ITERS, NZ * NY, 2, LANES), F32),
        vmem((ITERS, 24, LANES), F32),
        vmem((ITERS, NX * NC, 24, LANES), F32),
        vmem((ITERS, 16, LANES), BF16),
        vmem((ITERS, GROUPS, 16, LANES), BF16),
        vmem((1, 1, LANES), F32),
        vmem((NZ * NY, 1, LANES), F32),
        vmem((1, 1, LANES), F32),
        vmem((NX * NC, 1, LANES), F32),
        vmem((1, LANES), F32),
        dma((8,)), dma,
        dma((ITERS,)), dma((ITERS,)), dma((ITERS,)), dma((ITERS,)),
        dma((ITERS,)), dma((ITERS,)), dma((ITERS,)),
        dma((ITERS, GROUPS)),
        dma, dma, dma, dma,
    ]
    u, row = pl.pallas_call(
        kernel,
        out_shape=(
            jax.ShapeDtypeStruct((16, 768), F32),
            jax.ShapeDtypeStruct((1, LANES), F32),
        ),
        in_specs=[pl.BlockSpec(memory_space=pl.ANY)] * 8,
        out_specs=(
            pl.BlockSpec(memory_space=pl.ANY),
            pl.BlockSpec(memory_space=pltpu.VMEM),
        ),
        scratch_shapes=scratch,
        compiler_params=pltpu.CompilerParams(
            collective_id=0, has_side_effects=True, vmem_limit_bytes=56 << 20
        ),
        name="relaxation",
    )(
        displacement,
        surface_load,
        dens_grad,
        dens_ref.reshape(1, 16),
        relax_rate,
        basis,
        neighbours,
        green.reshape((DEG + 1) * L, L),
    )
    relaxed, sizes = pl.pallas_call(
        finish,
        out_shape=(
            jax.ShapeDtypeStruct((16, 768), F32),
            jax.ShapeDtypeStruct((1, ITERS), F32),
        ),
        in_specs=[
            pl.BlockSpec(memory_space=pl.ANY),
            pl.BlockSpec(memory_space=pltpu.VMEM),
        ],
        out_specs=(
            pl.BlockSpec(memory_space=pl.ANY),
            pl.BlockSpec(memory_space=pltpu.VMEM),
        ),
        scratch_shapes=[dma],
        name="finish",
    )(u, row)
    return relaxed, sizes.reshape(ITERS)


def solution(mesh):
    torus = Mesh(mesh.devices.reshape(NZ, NY, NC, NX), AXES)
    return jax.shard_map(
        local,
        mesh=torus,
        in_specs=(
            P("rad", LAT),
            P("rad", LAT),
            P("rad", LAT),
            P("rad"),
            P("rad", LAT),
            P(None, LAT),
            P(None, LAT),
            P(),
        ),
        out_specs=(P("rad", LAT), P()),
        check_vma=False,
    )
```

```python
import jax
import jax.numpy as jnp
from jax import lax
from jax.experimental import pallas as pl
from jax.experimental.pallas import tpu as pltpu
from jax.sharding import Mesh
from jax.sharding import PartitionSpec as P

DEG = 48
L = 64
ITERS = 3
KH = 2401
NZ, NY, NC, NX = 8, 8, 2, 4
GROUPS = 19
LANES = 128
AXES = ("lz", "ly", "lc", "rad")
LAT = AXES[:3]
MESH = pl.DeviceIdType.MESH
NT = (((1,), (1,)), ((), ()))
NN = (((1,), (0,)), ((), ()))
F32 = jnp.float32
BF16 = jnp.bfloat16

PLANE = sorted(
    [(dz, dy) for dz in range(NZ) for dy in range(NY) if dz or dy],
    key=lambda o: -(min(o[0], NZ - o[0]) + min(o[1], NY - o[1])),
)


def group_chip(g):
    if g < 8:
        return g, g % 4
    if g < 16:
        return g - 8, (g - 8 + 2) % 4
    return (g - 16) * 3, ((g - 16) * 3 + 1) % 4


def owned_group(z, y, core):
    b = y // 2
    g = jnp.where(b == z % 4, z, -1)
    g = jnp.where(b == (z + 2) % 4, z + 8, g)
    extra = (b == (z + 1) % 4) & (z % 3 == 0)
    g = jnp.where(extra, z // 3 + 16, g)
    return jnp.where(y % 2 == core, g, -1)


def kernel(
    disp, load, grad, dref, rate, basis_hbm, nbr, green_hbm,
    out, sizes,
    basis, green, u_s, ld_s, rt_s, gr_s, nbr_s, dref_s, count, gexp, onehot,
    base, part, edge, rsbuf, edgebuf, xsend, xbuf, lsend, lbuf, fsend, fplane, fsend2, fx, sq_s, delta_s,
    in_sem, out_sem, rs_ssem, rs_rsem, e_ssem, e_rsem, x_ssem, x_rsem, ag_ssem, ag_rsem,
    f_ssem, f_rsem, f2_ssem, f2_rsem,
):
    z, y, c, x = (lax.axis_index(a) for a in AXES)
    chip = z * NY + y
    g_own = owned_group(z, y, c)
    owner = g_own >= 0
    other_y = 2 * (y // 2) + (1 - y % 2)

    plane_ids = [((z + dz) % NZ, (y + dy) % NY, c, x) for dz, dy in PLANE]
    same = [(z, y, c, (x + d) % NX) for d in (2, 1, 3)]
    cross = [(z, other_y, 1 - c, (x + d) % NX) for d in (2, 1, 3, 0)]
    near_ids = same + cross

    barrier = pltpu.get_barrier_semaphore()
    for dev in plane_ids + near_ids:
        pl.semaphore_signal(barrier, inc=1, device_id=dev, device_id_type=MESH)

    loads = [
        pltpu.make_async_copy(disp, u_s, in_sem.at[0]),
        pltpu.make_async_copy(grad, gr_s, in_sem.at[1]),
        pltpu.make_async_copy(dref, dref_s, in_sem.at[2]),
        pltpu.make_async_copy(basis_hbm, basis, in_sem.at[3]),
        pltpu.make_async_copy(nbr, nbr_s, in_sem.at[4]),
        pltpu.make_async_copy(green_hbm, green, in_sem.at[5]),
        pltpu.make_async_copy(load, ld_s, in_sem.at[6]),
        pltpu.make_async_copy(rate, rt_s, in_sem.at[7]),
    ]
    for copy in loads:
        copy.start()

    def count_rows(block, carry):
        start = pl.multiple_of(block * 64, 64)
        rows = lax.broadcasted_iota(jnp.int32, (64, 768), 0) + start
        total = jnp.zeros((64, 768), F32)
        for j in range(4):
            total = total + jnp.where(nbr_s[j : j + 1, :] == rows, 1.0, 0.0)
        count[pl.ds(start, 64), :] = total.astype(BF16)
        return carry

    def green_row(i):
        layer = x * 16 + i
        inside = (layer >= 0) & (layer < L)
        at = jnp.where(inside, layer, 0)
        rows = green[pl.ds(at, DEG + 1, stride=L), :]
        rows = jnp.where(inside, rows, 0.0)
        return jnp.concatenate([rows, jnp.zeros((64 - DEG - 1, L), F32)], axis=0)

    def expand(i, carry):
        diff = ((green_row(i + 1) - green_row(i - 1)) * 0.5).T
        high = diff.astype(BF16).astype(F32)
        both = jnp.concatenate([high, diff - high], axis=1).astype(BF16)
        gexp[i] = lax.dot_general(both, onehot[...], NN, preferred_element_type=F32)
        return carry

    for copy in loads[:4]:
        copy.wait()
    eye = lax.broadcasted_iota(jnp.int32, (16, 16), 0) == lax.broadcasted_iota(jnp.int32, (16, 16), 1)
    half_ref = 0.5 * jnp.sum(jnp.where(eye, dref_s[...], 0.0), axis=1, keepdims=True)
    ends = jnp.concatenate(
        [
            jnp.broadcast_to(half_ref[0:1], (1, LANES)),
            jnp.broadcast_to(half_ref[15:16], (1, LANES)),
            jnp.zeros((4, LANES), F32),
        ],
        axis=0,
    )
    sq_s[...] = jnp.zeros((1, LANES), F32)
    delta_s[...] = jnp.zeros((16, 768), F32)

    pl.semaphore_wait(barrier, len(plane_ids) + len(near_ids))

    def add_squares(it):
        square = delta_s[...] * delta_s[...]
        square = jnp.sum(jnp.sum(square, axis=0, keepdims=True), axis=1, keepdims=True)
        lane = lax.broadcasted_iota(jnp.int32, (1, LANES), 1)
        sq_s[...] = jnp.where(lane == it, square, sq_s[...])

    def step(it, carry):
        u = u_s[...]
        line = jnp.zeros((1, 768), F32)
        upper = jnp.concatenate([u[1:16], line], axis=0)
        lower = jnp.concatenate([line, u[0:15]], axis=0)
        rho = gr_s[...] * u + half_ref * (upper - lower)
        lines = jnp.concatenate([rho, u[0:1], u[15:16], jnp.zeros((14, 768), F32)], axis=0)
        lines = lines.astype(BF16)

        for g in range(GROUPS):
            tile = lax.dot_general(
                lines, basis[g * LANES : (g + 1) * LANES, :], NT, preferred_element_type=F32
            )
            part[it, g] = tile[0:16].astype(BF16)
            edge[it, g] = tile[16:18]
        for g in range(GROUPS):
            gz, gb = group_chip(g)
            dev = (gz, gb * 2 + c, c, x)

            @pl.when(g_own != g)
            def _():
                pltpu.make_async_remote_copy(
                    src_ref=part.at[it, g], dst_ref=rsbuf.at[it, chip],
                    send_sem=rs_ssem.at[it], recv_sem=rs_rsem.at[it],
                    device_id=dev, device_id_type=MESH,
                ).start()
                pltpu.make_async_remote_copy(
                    src_ref=edge.at[it, g], dst_ref=edgebuf.at[it, chip],
                    send_sem=e_ssem.at[it], recv_sem=e_rsem.at[it],
                    device_id=dev, device_id_type=MESH,
                ).start()

        @pl.when(it == 0)
        def _():
            for copy in loads[4:]:
                copy.wait()
            lax.fori_loop(0, 12, count_rows, 0)

            @pl.when(owner)
            def _():
                k = g_own * LANES + lax.broadcasted_iota(jnp.int32, (LANES, LANES), 1)
                d = lax.broadcasted_iota(jnp.int32, (LANES, LANES), 0) % 64
                hit = (k >= d * d) & (k < (d + 1) * (d + 1)) & (k < KH)
                onehot[...] = jnp.where(hit, 1.0, 0.0).astype(BF16)
                lax.fori_loop(0, 16, expand, 0)

        high = u.astype(BF16).astype(F32)
        halves = jnp.concatenate([high, u - high], axis=0).astype(BF16)
        gathered = lax.dot_general(halves, count[...], NN, preferred_element_type=F32)
        lap = gathered[0:16] + gathered[16:32] - 4.0 * u
        base[...] = ld_s[...] + lap - u

        add_squares(it - 1)

        @pl.when(owner)
        def _():
            rsbuf[it, chip] = part[it, g_own]
            edgebuf[it, chip] = edge[it, g_own]
            incoming = rsbuf.at[it, pl.ds(0, NZ * NY - 1)]
            pltpu.make_async_copy(incoming, incoming, rs_rsem.at[it]).wait()
            sums = [jnp.zeros((16, LANES), F32) for _ in range(4)]
            for s in range(NZ * NY):
                sums[s % 4] = sums[s % 4] + rsbuf[it, s].astype(F32)
            total = (sums[0] + sums[1]) + (sums[2] + sums[3])
            edges = edgebuf.at[it, pl.ds(0, NZ * NY - 1)]
            pltpu.make_async_copy(edges, edges, e_rsem.at[it]).wait()
            sums = [jnp.zeros((2, LANES), F32) for _ in range(4)]
            for s in range(NZ * NY):
                sums[s % 4] = sums[s % 4] + edgebuf[it, s]
            edge_total = (sums[0] + sums[1]) + (sums[2] + sums[3])
            total = jnp.concatenate([total, edge_total, ends], axis=0)
            xsend[it] = total
            me = x * NC + c
            for dev in near_ids:
                pltpu.make_async_remote_copy(
                    src_ref=xsend.at[it], dst_ref=xbuf.at[it, me],
                    send_sem=x_ssem.at[it], recv_sem=x_rsem.at[it],
                    device_id=dev, device_id_type=MESH,
                ).start()
            xbuf[it, me] = total
            others = xbuf.at[it, pl.ds(0, NX * NC - 1)]
            pltpu.make_async_copy(others, others, x_rsem.at[it]).wait()
            blocks = [xbuf[it, 2 * b] + xbuf[it, 2 * b + 1] for b in range(NX)]
            rows = []
            for b in range(NX):
                first, last = jnp.zeros((1, LANES), F32), jnp.zeros((1, LANES), F32)
                if b > 0:
                    first = -0.5 * blocks[b][18:19] * blocks[b - 1][17:18]
                if b < NX - 1:
                    last = 0.5 * blocks[b][19:20] * blocks[b + 1][16:17]
                mid = jnp.zeros((14, LANES), F32)
                rows.append(blocks[b][0:16] + jnp.concatenate([first, mid, last], axis=0))
            coefs = jnp.concatenate(rows, axis=0)
            rows = [jnp.sum(gexp[i] * coefs, axis=0, keepdims=True) for i in range(16)]
            phi = jnp.concatenate(rows, axis=0).astype(BF16)
            lsend[it] = phi
            for dev in plane_ids:
                pltpu.make_async_remote_copy(
                    src_ref=lsend.at[it], dst_ref=lbuf.at[it, g_own],
                    send_sem=ag_ssem.at[it], recv_sem=ag_rsem.at[it, g_own],
                    device_id=dev, device_id_type=MESH,
                ).start()
            lbuf[it, g_own] = phi

        force = jnp.zeros((16, 768), F32)
        for groups in (range(0, 10), range(10, GROUPS)):
            for g in groups:
                @pl.when(g_own != g)
                def _():
                    pltpu.make_async_copy(lbuf.at[it, g], lbuf.at[it, g], ag_rsem.at[it, g]).wait()
            for g in groups:
                force = force + lax.dot_general(
                    lbuf[it, g], basis[g * LANES : (g + 1) * LANES, :], NN,
                    preferred_element_type=F32,
                )
        delta = rt_s[...] * (base[...] + force)
        delta_s[...] = delta
        u_s[...] = u + delta
        return carry

    lax.fori_loop(0, ITERS, step, 0)
    result = pltpu.make_async_copy(u_s, out, out_sem)
    result.start()

    add_squares(ITERS - 1)
    fsend[0] = sq_s[...]
    for dev in plane_ids:
        pltpu.make_async_remote_copy(
            src_ref=fsend.at[0], dst_ref=fplane.at[chip], send_sem=f_ssem, recv_sem=f_rsem,
            device_id=dev, device_id_type=MESH,
        ).start()
    fplane[chip] = sq_s[...]
    others = fplane.at[pl.ds(0, NZ * NY - 1)]
    pltpu.make_async_copy(others, others, f_rsem).wait()
    total = jnp.zeros((1, LANES), F32)
    for s in range(NZ * NY):
        total = total + fplane[s]
    fsend2[0] = total
    me = x * NC + c
    for dev in near_ids:
        pltpu.make_async_remote_copy(
            src_ref=fsend2.at[0], dst_ref=fx.at[me], send_sem=f2_ssem, recv_sem=f2_rsem,
            device_id=dev, device_id_type=MESH,
        ).start()
    fx[me] = total
    others2 = fx.at[pl.ds(0, NX * NC - 1)]
    pltpu.make_async_copy(others2, others2, f2_rsem).wait()
    total = jnp.zeros((1, LANES), F32)
    for s in range(NX * NC):
        total = total + fx[s]
    sizes[...] = jnp.sqrt(total * (1.0 / (L * 768 * NZ * NY * NC)))[:, 0:ITERS]

    result.wait()
    pltpu.make_async_copy(others, others, f_ssem).wait()
    pltpu.make_async_copy(others2, others2, f2_ssem).wait()
    for it in range(ITERS):
        @pl.when(owner)
        def _():
            sent = part.at[it, pl.ds(0, GROUPS - 1)]
            pltpu.make_async_copy(sent, sent, rs_ssem.at[it]).wait()
            sent = xbuf.at[it, pl.ds(0, NX * NC - 1)]
            pltpu.make_async_copy(sent, sent, x_ssem.at[it]).wait()
            sent = edge.at[it, pl.ds(0, GROUPS - 1)]
            pltpu.make_async_copy(sent, sent, e_ssem.at[it]).wait()
            sent = rsbuf.at[0, pl.ds(0, NZ * NY - 1)]
            pltpu.make_async_copy(sent, sent, ag_ssem.at[it]).wait()

        @pl.when(jnp.logical_not(owner))
        def _():
            sent = part.at[it]
            pltpu.make_async_copy(sent, sent, rs_ssem.at[it]).wait()
            sent = edge.at[it]
            pltpu.make_async_copy(sent, sent, e_ssem.at[it]).wait()


def local(displacement, surface_load, dens_grad, dens_ref, relax_rate, basis, neighbours, green):
    vmem = pltpu.VMEM
    dma = pltpu.SemaphoreType.DMA
    scratch = [
        vmem((2432, 768), BF16),
        vmem(((DEG + 1) * L, L), F32),
        vmem((16, 768), F32),
        vmem((16, 768), F32),
        vmem((16, 768), F32),
        vmem((16, 768), F32),
        vmem((4, 768), jnp.int32),
        vmem((1, 16), F32),
        vmem((768, 768), BF16),
        vmem((16, 64, LANES), F32),
        vmem((LANES, LANES), BF16),
        vmem((16, 768), F32),
        vmem((ITERS, GROUPS, 16, LANES), BF16),
        vmem((ITERS, GROUPS, 2, LANES), F32),
        vmem((ITERS, NZ * NY, 16, LANES), BF16),
        vmem((ITERS, NZ * NY, 2, LANES), F32),
        vmem((ITERS, 24, LANES), F32),
        vmem((ITERS, NX * NC, 24, LANES), F32),
        vmem((ITERS, 16, LANES), BF16),
        vmem((ITERS, GROUPS, 16, LANES), BF16),
        vmem((1, 1, LANES), F32),
        vmem((NZ * NY, 1, LANES), F32),
        vmem((1, 1, LANES), F32),
        vmem((NX * NC, 1, LANES), F32),
        vmem((1, LANES), F32),
        vmem((16, 768), F32),
        dma((8,)), dma,
        dma((ITERS,)), dma((ITERS,)), dma((ITERS,)), dma((ITERS,)),
        dma((ITERS,)), dma((ITERS,)), dma((ITERS,)),
        dma((ITERS, GROUPS)),
        dma, dma, dma, dma,
    ]
    relaxed, sizes = pl.pallas_call(
        kernel,
        out_shape=(
            jax.ShapeDtypeStruct((16, 768), F32),
            jax.ShapeDtypeStruct((1, ITERS), F32),
        ),
        in_specs=[pl.BlockSpec(memory_space=pl.ANY)] * 8,
        out_specs=(
            pl.BlockSpec(memory_space=pl.ANY),
            pl.BlockSpec(memory_space=pltpu.VMEM),
        ),
        scratch_shapes=scratch,
        compiler_params=pltpu.CompilerParams(
            collective_id=0, has_side_effects=True, vmem_limit_bytes=56 << 20
        ),
        name="relaxation",
    )(
        displacement,
        surface_load,
        dens_grad,
        dens_ref.reshape(1, 16),
        relax_rate,
        basis,
        neighbours,
        green.reshape((DEG + 1) * L, L),
    )
    return relaxed, sizes.reshape(ITERS)


def solution(mesh):
    torus = Mesh(mesh.devices.reshape(NZ, NY, NC, NX), AXES)
    return jax.shard_map(
        local,
        mesh=torus,
        in_specs=(
            P("rad", LAT),
            P("rad", LAT),
            P("rad", LAT),
            P("rad"),
            P("rad", LAT),
            P(None, LAT),
            P(None, LAT),
            P(),
        ),
        out_specs=(P("rad", LAT), P()),
        check_vma=False,
    )
```

```python
import jax
import jax.numpy as jnp
from jax import lax
from jax.experimental import pallas as pl
from jax.experimental.pallas import tpu as pltpu
from jax.sharding import Mesh
from jax.sharding import PartitionSpec as P

DEG = 48
L = 64
ITERS = 3
KH = 2401
NZ, NY, NC, NX = 8, 8, 2, 4
GROUPS = 19
LANES = 128
AXES = ("lz", "ly", "lc", "rad")
LAT = AXES[:3]
LOGICAL = pl.DeviceIdType.LOGICAL
NT = (((1,), (1,)), ((), ()))
NN = (((1,), (0,)), ((), ()))
F32 = jnp.float32
BF16 = jnp.bfloat16

PLANE = sorted(
    [(dz, dy) for dz in range(NZ) for dy in range(NY) if dz or dy],
    key=lambda o: -(min(o[0], NZ - o[0]) + min(o[1], NY - o[1])),
)


def distance(o):
    return min(o[0], NZ - o[0]) + min(o[1], NY - o[1])


SERVED = [
    o for o in [*PLANE, (0, 0)] if distance(o) < 4 or (distance(o) == 4 and o[0] < 4)
]
assert len(SERVED) == NZ * NY // 2


def group_chip(g):
    return g % 4, (3 * (g // 4) + 2 * (g % 4)) % NY


def owned_group(z, y, core):
    half_z, half_y = z & 3, (y - core + (z & 4)) & 7
    owned = jnp.int32(-1)
    for g in range(GROUPS):
        gz, gy = group_chip(g)
        owned = jnp.where((half_z == gz) & (half_y == gy), g, owned)
    return owned


def kernel(
    disp, load, grad, dref, rate, basis_hbm, nbr, green_hbm,
    out, sizes,
    basis, green, u_s, ld_s, rt_s, gr_s, nbr_s, dref_s, count, gexp, onehot,
    base, part, edge, rsbuf, edgebuf, xsend, xbuf, csend, cbuf, cedge, cedgebuf, lsend, lbuf, fsend, frow, fsend2, fz, sq_s, delta_s,
    in_sem, out_sem, rs_ssem, rs_rsem, e_ssem, e_rsem, x_ssem, x_rsem, c_ssem, c_rsem, ce_ssem, ce_rsem, ag_ssem, ag_rsem,
    f_ssem, f_rsem, f2_ssem, f2_rsem,
):
    z, y, c, x = (lax.axis_index(a) for a in AXES)
    chip = z * NY + y
    g_own = owned_group(z, y, c)
    owner = g_own >= 0
    other_y = (y + 1 - 2 * c) & 7
    site_z = z & 4

    own_lane = c * 4 + x
    z_part = [((z + d) & 7) * 64 for d in range(NZ)]
    y_part = [((y + d) & 7) * 8 + own_lane for d in range(NY)]
    plane_ids = [z_part[dz] + y_part[dy] for dz, dy in PLANE]
    served_ids = [z_part[dz] + y_part[dy] for dz, dy in SERVED[:-1]]
    same = [z_part[0] + y_part[0] - x + ((x + d) & 3) for d in (2, 1, 3)]
    cross = [z_part[0] + other_y * 8 + (1 - c) * 4 + ((x + d) & 3) for d in (2, 1, 3, 0)]
    row_ids = [
        z_part[0] + (y_part[dy] ^ bits) for dy in (4, 3, 5, 2, 6, 1, 7, 0)
        for bits in (2, 6, 1, 3, 5, 7, 4, 0) if dy or bits
    ]
    column_ids = [z_part[dz] + y_part[0] for dz in (4, 3, 5, 2, 6, 1, 7)]

    greeted_ids = [
        z_part[0] + (y_part[dy] ^ bits) for dy in (4, 3, 5, 2, 6, 1, 7, 0) for bits in range(1, 8)
    ]
    barrier = pltpu.get_barrier_semaphore()
    for dev in plane_ids + greeted_ids:
        pl.semaphore_signal(barrier, inc=1, device_id=dev, device_id_type=LOGICAL)

    loads = [
        pltpu.make_async_copy(disp, u_s, in_sem.at[0]),
        pltpu.make_async_copy(grad, gr_s, in_sem.at[1]),
        pltpu.make_async_copy(dref, dref_s, in_sem.at[2]),
        pltpu.make_async_copy(basis_hbm, basis, in_sem.at[3]),
        pltpu.make_async_copy(nbr, nbr_s, in_sem.at[4]),
        pltpu.make_async_copy(green_hbm, green, in_sem.at[5]),
        pltpu.make_async_copy(load, ld_s, in_sem.at[6]),
        pltpu.make_async_copy(rate, rt_s, in_sem.at[7]),
    ]
    for copy in loads:
        copy.start()

    def count_rows(block, carry):
        start = pl.multiple_of(block * 64, 64)
        rows = lax.broadcasted_iota(jnp.int32, (64, 768), 0) + start
        total = jnp.zeros((64, 768), F32)
        for j in range(4):
            total = total + jnp.where(nbr_s[j : j + 1, :] == rows, 1.0, 0.0)
        count[pl.ds(start, 64), :] = total.astype(BF16)
        return carry

    def green_row(i):
        layer = x * 16 + i
        inside = (layer >= 0) & (layer < L)
        at = jnp.where(inside, layer, 0)
        rows = green[pl.ds(at, DEG + 1, stride=L), :]
        rows = jnp.where(inside, rows, 0.0)
        return jnp.concatenate([rows, jnp.zeros((64 - DEG - 1, L), F32)], axis=0)

    def expand(i, carry):
        diff = ((green_row(i + 1) - green_row(i - 1)) * 0.5).T
        high = diff.astype(BF16).astype(F32)
        both = jnp.concatenate([high, diff - high], axis=1).astype(BF16)
        gexp[i] = lax.dot_general(both, onehot[...], NN, preferred_element_type=F32)
        return carry

    for copy in loads[:4]:
        copy.wait()
    eye = lax.broadcasted_iota(jnp.int32, (16, 16), 0) == lax.broadcasted_iota(jnp.int32, (16, 16), 1)
    half_ref = 0.5 * jnp.sum(jnp.where(eye, dref_s[...], 0.0), axis=1, keepdims=True)
    ends = jnp.concatenate(
        [
            jnp.broadcast_to(half_ref[0:1], (1, LANES)),
            jnp.broadcast_to(half_ref[15:16], (1, LANES)),
            jnp.zeros((4, LANES), F32),
        ],
        axis=0,
    )
    sq_s[...] = jnp.zeros((1, LANES), F32)
    delta_s[...] = jnp.zeros((16, 768), F32)

    pl.semaphore_wait(barrier, len(plane_ids) + len(greeted_ids))

    def add_squares(it):
        square = delta_s[...] * delta_s[...]
        square = jnp.sum(jnp.sum(square, axis=0, keepdims=True), axis=1, keepdims=True)
        lane = lax.broadcasted_iota(jnp.int32, (1, LANES), 1)
        sq_s[...] = jnp.where(lane == it, square, sq_s[...])

    def step(it, carry):
        u = u_s[...]
        line = jnp.zeros((1, 768), F32)
        upper = jnp.concatenate([u[1:16], line], axis=0)
        lower = jnp.concatenate([line, u[0:15]], axis=0)
        rho = gr_s[...] * u + half_ref * (upper - lower)
        lines = jnp.concatenate([rho, u[0:1], u[15:16], jnp.zeros((14, 768), F32)], axis=0)
        lines = lines.astype(BF16)

        def send_groups(groups):
            for g in groups:
                gz, gy = group_chip(g)
                for at in range(2):
                    dev = (gz + 4 * at) * 64 + ((gy + 4 * at) % NY * 8 + c * 8 & 63) + own_lane

                    @pl.when((g_own != g) | (site_z != 4 * at))
                    def _():
                        pltpu.make_async_remote_copy(
                            src_ref=part.at[it, g], dst_ref=rsbuf.at[it, chip],
                            send_sem=rs_ssem.at[it], recv_sem=rs_rsem.at[it],
                            device_id=dev, device_id_type=LOGICAL,
                        ).start()
                        pltpu.make_async_remote_copy(
                            src_ref=edge.at[it, g], dst_ref=edgebuf.at[it, chip],
                            send_sem=e_ssem.at[it], recv_sem=e_rsem.at[it],
                            device_id=dev, device_id_type=LOGICAL,
                        ).start()

        for g in range(0, 10):
            tile = lax.dot_general(
                lines, basis[g * LANES : (g + 1) * LANES, :], NT, preferred_element_type=F32
            )
            part[it, g] = tile[0:16].astype(BF16)
            edge[it, g] = tile[16:18]
        send_groups(range(0, 10))
        for g in range(10, GROUPS):
            tile = lax.dot_general(
                lines, basis[g * LANES : (g + 1) * LANES, :], NT, preferred_element_type=F32
            )
            part[it, g] = tile[0:16].astype(BF16)
            edge[it, g] = tile[16:18]
        send_groups(range(10, GROUPS))

        @pl.when(it == 0)
        def _():
            for copy in loads[4:]:
                copy.wait()
            lax.fori_loop(0, 12, count_rows, 0)

            @pl.when(owner)
            def _():
                k = g_own * LANES + lax.broadcasted_iota(jnp.int32, (LANES, LANES), 1)
                d = lax.broadcasted_iota(jnp.int32, (LANES, LANES), 0) % 64
                hit = (k >= d * d) & (k < (d + 1) * (d + 1)) & (k < KH)
                onehot[...] = jnp.where(hit, 1.0, 0.0).astype(BF16)
                lax.fori_loop(0, 16, expand, 0)

        high = u.astype(BF16).astype(F32)
        halves = jnp.concatenate([high, u - high], axis=0).astype(BF16)
        gathered = lax.dot_general(halves, count[...], NN, preferred_element_type=F32)
        lap = gathered[0:16] + gathered[16:32] - 4.0 * u
        base[...] = ld_s[...] + lap - u

        add_squares(it - 1)

        @pl.when(owner)
        def _():
            rsbuf[it, chip] = part[it, g_own]
            edgebuf[it, chip] = edge[it, g_own]
            incoming = rsbuf.at[it, pl.ds(0, NZ * NY - 1)]
            pltpu.make_async_copy(incoming, incoming, rs_rsem.at[it]).wait()
            sums = [jnp.zeros((16, LANES), F32) for _ in range(4)]
            for s in range(NZ * NY):
                sums[s % 4] = sums[s % 4] + rsbuf[it, s].astype(F32)
            total = (sums[0] + sums[1]) + (sums[2] + sums[3])
            edges = edgebuf.at[it, pl.ds(0, NZ * NY - 1)]
            pltpu.make_async_copy(edges, edges, e_rsem.at[it]).wait()
            sums = [jnp.zeros((2, LANES), F32) for _ in range(4)]
            for s in range(NZ * NY):
                sums[s % 4] = sums[s % 4] + edgebuf[it, s]
            edge_total = (sums[0] + sums[1]) + (sums[2] + sums[3])
            own = jnp.concatenate([total, edge_total, ends], axis=0)
            xsend[it] = own
            csend[it] = total.astype(BF16)
            cedge[it] = edge_total
            for dev in same:
                pltpu.make_async_remote_copy(
                    src_ref=xsend.at[it], dst_ref=xbuf.at[it, x],
                    send_sem=x_ssem.at[it], recv_sem=x_rsem.at[it],
                    device_id=dev, device_id_type=LOGICAL,
                ).start()
            for dev in cross:
                pltpu.make_async_remote_copy(
                    src_ref=csend.at[it], dst_ref=cbuf.at[it, x],
                    send_sem=c_ssem.at[it], recv_sem=c_rsem.at[it],
                    device_id=dev, device_id_type=LOGICAL,
                ).start()
                pltpu.make_async_remote_copy(
                    src_ref=cedge.at[it], dst_ref=cedgebuf.at[it, x],
                    send_sem=ce_ssem.at[it], recv_sem=ce_rsem.at[it],
                    device_id=dev, device_id_type=LOGICAL,
                ).start()
            xbuf[it, x] = own
            others = xbuf.at[it, pl.ds(0, NX - 1)]
            pltpu.make_async_copy(others, others, x_rsem.at[it]).wait()
            pltpu.make_async_copy(cbuf.at[it], cbuf.at[it], c_rsem.at[it]).wait()
            pltpu.make_async_copy(cedgebuf.at[it], cedgebuf.at[it], ce_rsem.at[it]).wait()
            blocks = [xbuf[it, b, 0:16] + cbuf[it, b].astype(F32) for b in range(NX)]
            outer = [xbuf[it, b, 16:18] + cedgebuf[it, b] for b in range(NX)]
            rows = []
            for b in range(NX):
                first, last = jnp.zeros((1, LANES), F32), jnp.zeros((1, LANES), F32)
                if b > 0:
                    first = -xbuf[it, b, 18:19] * outer[b - 1][1:2]
                if b < NX - 1:
                    last = xbuf[it, b, 19:20] * outer[b + 1][0:1]
                mid = jnp.zeros((14, LANES), F32)
                rows.append(blocks[b] + jnp.concatenate([first, mid, last], axis=0))
            coefs = jnp.concatenate(rows, axis=0)
            rows = [jnp.sum(gexp[i] * coefs, axis=0, keepdims=True) for i in range(16)]
            phi = jnp.concatenate(rows, axis=0).astype(BF16)
            lsend[it] = phi
            for dev in served_ids:
                pltpu.make_async_remote_copy(
                    src_ref=lsend.at[it], dst_ref=lbuf.at[it, g_own],
                    send_sem=ag_ssem.at[it], recv_sem=ag_rsem.at[it, g_own],
                    device_id=dev, device_id_type=LOGICAL,
                ).start()
            lbuf[it, g_own] = phi

        force = jnp.zeros((16, 768), F32)
        for groups in (range(0, 10), range(10, GROUPS)):
            for g in groups:
                @pl.when(g_own != g)
                def _():
                    pltpu.make_async_copy(lbuf.at[it, g], lbuf.at[it, g], ag_rsem.at[it, g]).wait()
            for g in groups:
                force = force + lax.dot_general(
                    lbuf[it, g], basis[g * LANES : (g + 1) * LANES, :], NN,
                    preferred_element_type=F32,
                )
        delta = rt_s[...] * (base[...] + force)
        delta_s[...] = delta
        u_s[...] = u + delta
        return carry

    lax.fori_loop(0, ITERS, step, 0)
    result = pltpu.make_async_copy(u_s, out, out_sem)
    result.start()

    add_squares(ITERS - 1)
    fsend[0] = sq_s[...]
    me = y * 8 + c * 4 + x
    for dev in row_ids:
        pltpu.make_async_remote_copy(
            src_ref=fsend.at[0], dst_ref=frow.at[me], send_sem=f_ssem, recv_sem=f_rsem,
            device_id=dev, device_id_type=LOGICAL,
        ).start()
    frow[me] = sq_s[...]
    others = frow.at[pl.ds(0, NY * NC * NX - 1)]
    pltpu.make_async_copy(others, others, f_rsem).wait()
    total = jnp.zeros((1, LANES), F32)
    for s in range(NY * NC * NX):
        total = total + frow[s]
    fsend2[0] = total
    for dev in column_ids:
        pltpu.make_async_remote_copy(
            src_ref=fsend2.at[0], dst_ref=fz.at[z], send_sem=f2_ssem, recv_sem=f2_rsem,
            device_id=dev, device_id_type=LOGICAL,
        ).start()
    fz[z] = total
    others2 = fz.at[pl.ds(0, NZ - 1)]
    pltpu.make_async_copy(others2, others2, f2_rsem).wait()
    total = jnp.zeros((1, LANES), F32)
    for s in range(NZ):
        total = total + fz[s]
    sizes[...] = jnp.sqrt(total * (1.0 / (L * 768 * NZ * NY * NC)))[:, 0:ITERS]

    result.wait()
    pltpu.make_async_copy(others, others, f_ssem).wait()
    pltpu.make_async_copy(others2, others2, f2_ssem).wait()
    for it in range(ITERS):
        @pl.when(owner)
        def _():
            sent = rsbuf.at[0, pl.ds(0, 2 * GROUPS - 1)]
            pltpu.make_async_copy(sent, sent, rs_ssem.at[it]).wait()
            sent = xbuf.at[it, pl.ds(0, NX - 1)]
            pltpu.make_async_copy(sent, sent, x_ssem.at[it]).wait()
            pltpu.make_async_copy(cbuf.at[it], cbuf.at[it], c_ssem.at[it]).wait()
            pltpu.make_async_copy(cedgebuf.at[it], cedgebuf.at[it], ce_ssem.at[it]).wait()
            sent = edgebuf.at[0, pl.ds(0, 2 * GROUPS - 1)]
            pltpu.make_async_copy(sent, sent, e_ssem.at[it]).wait()
            sent = rsbuf.at[0, pl.ds(0, NZ * NY // 2 - 1)]
            pltpu.make_async_copy(sent, sent, ag_ssem.at[it]).wait()

        @pl.when(jnp.logical_not(owner))
        def _():
            sent = rsbuf.at[0, pl.ds(0, 2 * GROUPS)]
            pltpu.make_async_copy(sent, sent, rs_ssem.at[it]).wait()
            sent = edgebuf.at[0, pl.ds(0, 2 * GROUPS)]
            pltpu.make_async_copy(sent, sent, e_ssem.at[it]).wait()


def local(displacement, surface_load, dens_grad, dens_ref, relax_rate, basis, neighbours, green):
    vmem = pltpu.VMEM
    dma = pltpu.SemaphoreType.DMA
    scratch = [
        vmem((2432, 768), BF16),
        vmem(((DEG + 1) * L, L), F32),
        vmem((16, 768), F32),
        vmem((16, 768), F32),
        vmem((16, 768), F32),
        vmem((16, 768), F32),
        vmem((4, 768), jnp.int32),
        vmem((1, 16), F32),
        vmem((768, 768), BF16),
        vmem((16, 64, LANES), F32),
        vmem((LANES, LANES), BF16),
        vmem((16, 768), F32),
        vmem((ITERS, GROUPS, 16, LANES), BF16),
        vmem((ITERS, GROUPS, 2, LANES), F32),
        vmem((ITERS, NZ * NY, 16, LANES), BF16),
        vmem((ITERS, NZ * NY, 2, LANES), F32),
        vmem((ITERS, 24, LANES), F32),
        vmem((ITERS, NX, 24, LANES), F32),
        vmem((ITERS, 16, LANES), BF16),
        vmem((ITERS, NX, 16, LANES), BF16),
        vmem((ITERS, 2, LANES), F32),
        vmem((ITERS, NX, 2, LANES), F32),
        vmem((ITERS, 16, LANES), BF16),
        vmem((ITERS, GROUPS, 16, LANES), BF16),
        vmem((1, 1, LANES), F32),
        vmem((NZ * NY, 1, LANES), F32),
        vmem((1, 1, LANES), F32),
        vmem((NZ, 1, LANES), F32),
        vmem((1, LANES), F32),
        vmem((16, 768), F32),
        dma((8,)), dma,
        dma((ITERS,)), dma((ITERS,)), dma((ITERS,)), dma((ITERS,)),
        dma((ITERS,)), dma((ITERS,)), dma((ITERS,)), dma((ITERS,)),
        dma((ITERS,)), dma((ITERS,)), dma((ITERS,)),
        dma((ITERS, GROUPS)),
        dma, dma, dma, dma,
    ]
    relaxed, sizes = pl.pallas_call(
        kernel,
        out_shape=(
            jax.ShapeDtypeStruct((16, 768), F32),
            jax.ShapeDtypeStruct((1, ITERS), F32),
        ),
        in_specs=[pl.BlockSpec(memory_space=pl.ANY)] * 8,
        out_specs=(
            pl.BlockSpec(memory_space=pl.ANY),
            pl.BlockSpec(memory_space=pltpu.VMEM),
        ),
        scratch_shapes=scratch,
        compiler_params=pltpu.CompilerParams(
            collective_id=0, has_side_effects=True, vmem_limit_bytes=56 << 20
        ),
        name="relaxation",
    )(
        displacement,
        surface_load,
        dens_grad,
        dens_ref.reshape(1, 16),
        relax_rate,
        basis,
        neighbours,
        green.reshape((DEG + 1) * L, L),
    )
    return relaxed, sizes.reshape(ITERS)


def solution(mesh):
    torus = Mesh(mesh.devices.reshape(NZ, NY, NC, NX), AXES)
    return jax.shard_map(
        local,
        mesh=torus,
        in_specs=(
            P("rad", LAT),
            P("rad", LAT),
            P("rad", LAT),
            P("rad"),
            P("rad", LAT),
            P(None, LAT),
            P(None, LAT),
            P(),
        ),
        out_specs=(P("rad", LAT), P()),
        check_vma=False,
    )
```

```python
import jax
import jax.numpy as jnp
from jax import lax
from jax.experimental import pallas as pl
from jax.experimental.pallas import tpu as pltpu
from jax.sharding import Mesh
from jax.sharding import PartitionSpec as P

DEG = 48
L = 64
ITERS = 3
KH = 2401
NZ, NY, NC, NX = 8, 8, 2, 4
GROUPS = 19
LANES = 128
AXES = ("lz", "ly", "lc", "rad")
LAT = AXES[:3]
LOGICAL = pl.DeviceIdType.LOGICAL
NT = (((1,), (1,)), ((), ()))
NN = (((1,), (0,)), ((), ()))
F32 = jnp.float32
BF16 = jnp.bfloat16

PLANE = sorted(
    [(dz, dy) for dz in range(NZ) for dy in range(NY) if dz or dy],
    key=lambda o: -(min(o[0], NZ - o[0]) + min(o[1], NY - o[1])),
)


def distance(o):
    return min(o[0], NZ - o[0]) + min(o[1], NY - o[1])


SERVED = [
    o for o in [*PLANE, (0, 0)] if distance(o) < 4 or (distance(o) == 4 and o[0] < 4)
]
assert len(SERVED) == NZ * NY // 2


def group_chip(g):
    return g % 4, (3 * (g // 4) + 2 * (g % 4)) % NY


def owned_group(z, y, core):
    half_z, half_y = z & 3, (y - core + (z & 4)) & 7
    owned = jnp.int32(-1)
    for g in range(GROUPS):
        gz, gy = group_chip(g)
        owned = jnp.where((half_z == gz) & (half_y == gy), g, owned)
    return owned


def kernel(
    disp, load, grad, dref, rate, basis_hbm, nbr, green_hbm,
    out, sizes,
    basis, green, u_s, ld_s, rt_s, gr_s, nbr_s, dref_s, count, gexp, onehot,
    base, part, edge, rsbuf, edgebuf, xsend, xbuf, csend, cbuf, cedge, cedgebuf, lsend, lbuf, fsend, frow, fsend2, fz, sq_s, delta_s,
    in_sem, out_sem, rs_ssem, rs_rsem, e_ssem, e_rsem, x_ssem, x_rsem, c_ssem, c_rsem, ce_ssem, ce_rsem, ag_ssem, ag_rsem,
    f_ssem, f_rsem, f2_ssem, f2_rsem,
):
    z, y, c, x = (lax.axis_index(a) for a in AXES)
    chip = z * NY + y
    g_own = owned_group(z, y, c)
    owner = g_own >= 0
    other_y = (y + 1 - 2 * c) & 7
    site_z = z & 4

    own_lane = c * 4 + x
    z_part = [((z + d) & 7) * 64 for d in range(NZ)]
    y_part = [((y + d) & 7) * 8 + own_lane for d in range(NY)]
    plane_ids = [z_part[dz] + y_part[dy] for dz, dy in PLANE]
    served_ids = [z_part[dz] + y_part[dy] for dz, dy in SERVED[:-1]]
    same = [z_part[0] + y_part[0] - x + ((x + d) & 3) for d in (2, 1, 3)]
    cross = [z_part[0] + other_y * 8 + (1 - c) * 4 + ((x + d) & 3) for d in (2, 1, 3, 0)]
    row_ids = [
        z_part[0] + (y_part[dy] ^ bits) for dy in (4, 3, 5, 2, 6, 1, 7, 0)
        for bits in (2, 6, 1, 3, 5, 7, 4, 0) if dy or bits
    ]
    column_ids = [z_part[dz] + y_part[0] for dz in (4, 3, 5, 2, 6, 1, 7)]

    greeted_ids = [
        z_part[0] + (y_part[dy] ^ bits) for dy in (4, 3, 5, 2, 6, 1, 7, 0) for bits in range(1, 8)
    ]
    barrier = pltpu.get_barrier_semaphore()
    for dev in plane_ids + greeted_ids:
        pl.semaphore_signal(barrier, inc=1, device_id=dev, device_id_type=LOGICAL)

    loads = [
        pltpu.make_async_copy(disp, u_s, in_sem.at[0]),
        pltpu.make_async_copy(grad, gr_s, in_sem.at[1]),
        pltpu.make_async_copy(dref, dref_s, in_sem.at[2]),
        pltpu.make_async_copy(basis_hbm, basis, in_sem.at[3]),
        pltpu.make_async_copy(nbr, nbr_s, in_sem.at[4]),
        pltpu.make_async_copy(green_hbm, green, in_sem.at[5]),
        pltpu.make_async_copy(load, ld_s, in_sem.at[6]),
        pltpu.make_async_copy(rate, rt_s, in_sem.at[7]),
    ]
    for copy in loads:
        copy.start()

    def count_rows(block, carry):
        start = pl.multiple_of(block * 64, 64)
        rows = lax.broadcasted_iota(jnp.int32, (64, 768), 0) + start
        total = jnp.zeros((64, 768), F32)
        for j in range(4):
            total = total + jnp.where(nbr_s[j : j + 1, :] == rows, 1.0, 0.0)
        count[pl.ds(start, 64), :] = total.astype(BF16)
        return carry

    def green_row(i):
        layer = x * 16 + i
        inside = (layer >= 0) & (layer < L)
        at = jnp.where(inside, layer, 0)
        rows = green[pl.ds(at, DEG + 1, stride=L), :]
        rows = jnp.where(inside, rows, 0.0)
        return jnp.concatenate([rows, jnp.zeros((64 - DEG - 1, L), F32)], axis=0)

    def expand(i, carry):
        diff = ((green_row(i + 1) - green_row(i - 1)) * 0.5).T
        high = diff.astype(BF16).astype(F32)
        both = jnp.concatenate([high, diff - high], axis=1).astype(BF16)
        gexp[i] = lax.dot_general(both, onehot[...], NN, preferred_element_type=F32)
        return carry

    for copy in loads[:4]:
        copy.wait()
    eye = lax.broadcasted_iota(jnp.int32, (16, 16), 0) == lax.broadcasted_iota(jnp.int32, (16, 16), 1)
    half_ref = 0.5 * jnp.sum(jnp.where(eye, dref_s[...], 0.0), axis=1, keepdims=True)
    ends = jnp.concatenate(
        [
            jnp.broadcast_to(half_ref[0:1], (1, LANES)),
            jnp.broadcast_to(half_ref[15:16], (1, LANES)),
            jnp.zeros((4, LANES), F32),
        ],
        axis=0,
    )
    sq_s[...] = jnp.zeros((1, LANES), F32)
    delta_s[...] = jnp.zeros((16, 768), F32)

    pl.semaphore_wait(barrier, len(plane_ids) + len(greeted_ids))

    def add_squares(it):
        square = delta_s[...] * delta_s[...]
        square = jnp.sum(jnp.sum(square, axis=0, keepdims=True), axis=1, keepdims=True)
        lane = lax.broadcasted_iota(jnp.int32, (1, LANES), 1)
        sq_s[...] = jnp.where(lane == it, square, sq_s[...])

    def step(it, carry):
        u = u_s[...]
        line = jnp.zeros((1, 768), F32)
        upper = jnp.concatenate([u[1:16], line], axis=0)
        lower = jnp.concatenate([line, u[0:15]], axis=0)
        rho = gr_s[...] * u + half_ref * (upper - lower)
        lines = jnp.concatenate([rho, u[0:1], u[15:16], jnp.zeros((14, 768), F32)], axis=0)
        lines = lines.astype(BF16)

        def send_groups(groups):
            for g in groups:
                gz, gy = group_chip(g)
                for at in range(2):
                    dev = (gz + 4 * at) * 64 + ((gy + 4 * at) % NY * 8 + c * 8 & 63) + own_lane

                    @pl.when((g_own != g) | (site_z != 4 * at))
                    def _():
                        pltpu.make_async_remote_copy(
                            src_ref=part.at[it, g], dst_ref=rsbuf.at[it, chip],
                            send_sem=rs_ssem.at[it], recv_sem=rs_rsem.at[it],
                            device_id=dev, device_id_type=LOGICAL,
                        ).start()
                        pltpu.make_async_remote_copy(
                            src_ref=edge.at[it, g], dst_ref=edgebuf.at[it, chip],
                            send_sem=e_ssem.at[it], recv_sem=e_rsem.at[it],
                            device_id=dev, device_id_type=LOGICAL,
                        ).start()

        for g in range(0, 10):
            tile = lax.dot_general(
                lines, basis[g * LANES : (g + 1) * LANES, :], NT, preferred_element_type=F32
            )
            part[it, g] = tile[0:16].astype(BF16)
            edge[it, g] = tile[16:18]
        send_groups(range(0, 10))
        for g in range(10, GROUPS):
            tile = lax.dot_general(
                lines, basis[g * LANES : (g + 1) * LANES, :], NT, preferred_element_type=F32
            )
            part[it, g] = tile[0:16].astype(BF16)
            edge[it, g] = tile[16:18]
        send_groups(range(10, GROUPS))

        @pl.when(it == 0)
        def _():
            for copy in loads[4:]:
                copy.wait()
            lax.fori_loop(0, 12, count_rows, 0)

        high = u.astype(BF16).astype(F32)
        halves = jnp.concatenate([high, u - high], axis=0).astype(BF16)
        gathered = lax.dot_general(halves, count[...], NN, preferred_element_type=F32)
        lap = gathered[0:16] + gathered[16:32] - 4.0 * u
        base[...] = ld_s[...] + lap - u

        add_squares(it - 1)

        @pl.when(owner)
        def _():
            rsbuf[it, chip] = part[it, g_own]
            edgebuf[it, chip] = edge[it, g_own]
            incoming = rsbuf.at[it, pl.ds(0, NZ * NY - 1)]
            pltpu.make_async_copy(incoming, incoming, rs_rsem.at[it]).wait()
            sums = [jnp.zeros((16, LANES), F32) for _ in range(4)]
            for s in range(NZ * NY):
                sums[s % 4] = sums[s % 4] + rsbuf[it, s].astype(F32)
            total = (sums[0] + sums[1]) + (sums[2] + sums[3])
            edges = edgebuf.at[it, pl.ds(0, NZ * NY - 1)]
            pltpu.make_async_copy(edges, edges, e_rsem.at[it]).wait()
            sums = [jnp.zeros((2, LANES), F32) for _ in range(4)]
            for s in range(NZ * NY):
                sums[s % 4] = sums[s % 4] + edgebuf[it, s]
            edge_total = (sums[0] + sums[1]) + (sums[2] + sums[3])
            own = jnp.concatenate([total, edge_total, ends], axis=0)
            xsend[it] = own
            csend[it] = total.astype(BF16)
            cedge[it] = edge_total
            for dev in same:
                pltpu.make_async_remote_copy(
                    src_ref=xsend.at[it], dst_ref=xbuf.at[it, x],
                    send_sem=x_ssem.at[it], recv_sem=x_rsem.at[it],
                    device_id=dev, device_id_type=LOGICAL,
                ).start()
            for dev in cross:
                pltpu.make_async_remote_copy(
                    src_ref=csend.at[it], dst_ref=cbuf.at[it, x],
                    send_sem=c_ssem.at[it], recv_sem=c_rsem.at[it],
                    device_id=dev, device_id_type=LOGICAL,
                ).start()
                pltpu.make_async_remote_copy(
                    src_ref=cedge.at[it], dst_ref=cedgebuf.at[it, x],
                    send_sem=ce_ssem.at[it], recv_sem=ce_rsem.at[it],
                    device_id=dev, device_id_type=LOGICAL,
                ).start()
            xbuf[it, x] = own

            @pl.when(it == 0)
            def _():
                k = g_own * LANES + lax.broadcasted_iota(jnp.int32, (LANES, LANES), 1)
                d = lax.broadcasted_iota(jnp.int32, (LANES, LANES), 0) % 64
                hit = (k >= d * d) & (k < (d + 1) * (d + 1)) & (k < KH)
                onehot[...] = jnp.where(hit, 1.0, 0.0).astype(BF16)
                lax.fori_loop(0, 16, expand, 0, unroll=4)

            others = xbuf.at[it, pl.ds(0, NX - 1)]
            pltpu.make_async_copy(others, others, x_rsem.at[it]).wait()
            pltpu.make_async_copy(cbuf.at[it], cbuf.at[it], c_rsem.at[it]).wait()
            pltpu.make_async_copy(cedgebuf.at[it], cedgebuf.at[it], ce_rsem.at[it]).wait()
            blocks = [xbuf[it, b, 0:16] + cbuf[it, b].astype(F32) for b in range(NX)]
            outer = [xbuf[it, b, 16:18] + cedgebuf[it, b] for b in range(NX)]
            rows = []
            for b in range(NX):
                first, last = jnp.zeros((1, LANES), F32), jnp.zeros((1, LANES), F32)
                if b > 0:
                    first = -xbuf[it, b, 18:19] * outer[b - 1][1:2]
                if b < NX - 1:
                    last = xbuf[it, b, 19:20] * outer[b + 1][0:1]
                mid = jnp.zeros((14, LANES), F32)
                rows.append(blocks[b] + jnp.concatenate([first, mid, last], axis=0))
            coefs = jnp.concatenate(rows, axis=0)
            rows = [jnp.sum(gexp[i] * coefs, axis=0, keepdims=True) for i in range(16)]
            phi = jnp.concatenate(rows, axis=0).astype(BF16)
            lsend[it] = phi
            for dev in served_ids:
                pltpu.make_async_remote_copy(
                    src_ref=lsend.at[it], dst_ref=lbuf.at[it, g_own],
                    send_sem=ag_ssem.at[it], recv_sem=ag_rsem.at[it, g_own],
                    device_id=dev, device_id_type=LOGICAL,
                ).start()
            lbuf[it, g_own] = phi

        force = jnp.zeros((16, 768), F32)
        for groups in (range(0, 10), range(10, GROUPS)):
            for g in groups:
                @pl.when(g_own != g)
                def _():
                    pltpu.make_async_copy(lbuf.at[it, g], lbuf.at[it, g], ag_rsem.at[it, g]).wait()
            for g in groups:
                force = force + lax.dot_general(
                    lbuf[it, g], basis[g * LANES : (g + 1) * LANES, :], NN,
                    preferred_element_type=F32,
                )
        delta = rt_s[...] * (base[...] + force)
        delta_s[...] = delta
        u_s[...] = u + delta
        return carry

    lax.fori_loop(0, ITERS, step, 0)
    result = pltpu.make_async_copy(u_s, out, out_sem)
    result.start()

    add_squares(ITERS - 1)
    fsend[0] = sq_s[...]
    me = y * 8 + c * 4 + x
    for dev in row_ids:
        pltpu.make_async_remote_copy(
            src_ref=fsend.at[0], dst_ref=frow.at[me], send_sem=f_ssem, recv_sem=f_rsem,
            device_id=dev, device_id_type=LOGICAL,
        ).start()
    frow[me] = sq_s[...]
    others = frow.at[pl.ds(0, NY * NC * NX - 1)]
    pltpu.make_async_copy(others, others, f_rsem).wait()
    total = jnp.zeros((1, LANES), F32)
    for s in range(NY * NC * NX):
        total = total + frow[s]
    fsend2[0] = total
    for dev in column_ids:
        pltpu.make_async_remote_copy(
            src_ref=fsend2.at[0], dst_ref=fz.at[z], send_sem=f2_ssem, recv_sem=f2_rsem,
            device_id=dev, device_id_type=LOGICAL,
        ).start()
    fz[z] = total
    others2 = fz.at[pl.ds(0, NZ - 1)]
    pltpu.make_async_copy(others2, others2, f2_rsem).wait()
    total = jnp.zeros((1, LANES), F32)
    for s in range(NZ):
        total = total + fz[s]
    sizes[...] = jnp.sqrt(total * (1.0 / (L * 768 * NZ * NY * NC)))[:, 0:ITERS]

    result.wait()
    pltpu.make_async_copy(others, others, f_ssem).wait()
    pltpu.make_async_copy(others2, others2, f2_ssem).wait()
    for it in range(ITERS):
        @pl.when(owner)
        def _():
            sent = rsbuf.at[0, pl.ds(0, 2 * GROUPS - 1)]
            pltpu.make_async_copy(sent, sent, rs_ssem.at[it]).wait()
            sent = xbuf.at[it, pl.ds(0, NX - 1)]
            pltpu.make_async_copy(sent, sent, x_ssem.at[it]).wait()
            pltpu.make_async_copy(cbuf.at[it], cbuf.at[it], c_ssem.at[it]).wait()
            pltpu.make_async_copy(cedgebuf.at[it], cedgebuf.at[it], ce_ssem.at[it]).wait()
            sent = edgebuf.at[0, pl.ds(0, 2 * GROUPS - 1)]
            pltpu.make_async_copy(sent, sent, e_ssem.at[it]).wait()
            sent = rsbuf.at[0, pl.ds(0, NZ * NY // 2 - 1)]
            pltpu.make_async_copy(sent, sent, ag_ssem.at[it]).wait()

        @pl.when(jnp.logical_not(owner))
        def _():
            sent = rsbuf.at[0, pl.ds(0, 2 * GROUPS)]
            pltpu.make_async_copy(sent, sent, rs_ssem.at[it]).wait()
            sent = edgebuf.at[0, pl.ds(0, 2 * GROUPS)]
            pltpu.make_async_copy(sent, sent, e_ssem.at[it]).wait()


def local(displacement, surface_load, dens_grad, dens_ref, relax_rate, basis, neighbours, green):
    vmem = pltpu.VMEM
    dma = pltpu.SemaphoreType.DMA
    scratch = [
        vmem((2432, 768), BF16),
        vmem(((DEG + 1) * L, L), F32),
        vmem((16, 768), F32),
        vmem((16, 768), F32),
        vmem((16, 768), F32),
        vmem((16, 768), F32),
        vmem((4, 768), jnp.int32),
        vmem((1, 16), F32),
        vmem((768, 768), BF16),
        vmem((16, 64, LANES), F32),
        vmem((LANES, LANES), BF16),
        vmem((16, 768), F32),
        vmem((ITERS, GROUPS, 16, LANES), BF16),
        vmem((ITERS, GROUPS, 2, LANES), F32),
        vmem((ITERS, NZ * NY, 16, LANES), BF16),
        vmem((ITERS, NZ * NY, 2, LANES), F32),
        vmem((ITERS, 24, LANES), F32),
        vmem((ITERS, NX, 24, LANES), F32),
        vmem((ITERS, 16, LANES), BF16),
        vmem((ITERS, NX, 16, LANES), BF16),
        vmem((ITERS, 2, LANES), F32),
        vmem((ITERS, NX, 2, LANES), F32),
        vmem((ITERS, 16, LANES), BF16),
        vmem((ITERS, GROUPS, 16, LANES), BF16),
        vmem((1, 1, LANES), F32),
        vmem((NZ * NY, 1, LANES), F32),
        vmem((1, 1, LANES), F32),
        vmem((NZ, 1, LANES), F32),
        vmem((1, LANES), F32),
        vmem((16, 768), F32),
        dma((8,)), dma,
        dma((ITERS,)), dma((ITERS,)), dma((ITERS,)), dma((ITERS,)),
        dma((ITERS,)), dma((ITERS,)), dma((ITERS,)), dma((ITERS,)),
        dma((ITERS,)), dma((ITERS,)), dma((ITERS,)),
        dma((ITERS, GROUPS)),
        dma, dma, dma, dma,
    ]
    relaxed, sizes = pl.pallas_call(
        kernel,
        out_shape=(
            jax.ShapeDtypeStruct((16, 768), F32),
            jax.ShapeDtypeStruct((1, ITERS), F32),
        ),
        in_specs=[pl.BlockSpec(memory_space=pl.ANY)] * 8,
        out_specs=(
            pl.BlockSpec(memory_space=pl.ANY),
            pl.BlockSpec(memory_space=pltpu.VMEM),
        ),
        scratch_shapes=scratch,
        compiler_params=pltpu.CompilerParams(
            collective_id=0, has_side_effects=True, vmem_limit_bytes=56 << 20
        ),
        name="relaxation",
    )(
        displacement,
        surface_load,
        dens_grad,
        dens_ref.reshape(1, 16),
        relax_rate,
        basis,
        neighbours,
        green.reshape((DEG + 1) * L, L),
    )
    return relaxed, sizes.reshape(ITERS)


def solution(mesh):
    torus = Mesh(mesh.devices.reshape(NZ, NY, NC, NX), AXES)
    return jax.shard_map(
        local,
        mesh=torus,
        in_specs=(
            P("rad", LAT),
            P("rad", LAT),
            P("rad", LAT),
            P("rad"),
            P("rad", LAT),
            P(None, LAT),
            P(None, LAT),
            P(),
        ),
        out_specs=(P("rad", LAT), P()),
        check_vma=False,
    )
```
